256 devices in a mesh: grp: 8 (over z_hi, y), seg: 32 (over z_lo, x, core).
Axes of the slice: x: 4, y: 4, z: 8 (z_hi: 2, z_lo: 4; z = z_hi * 4 + z_lo), core: 2. Of those that a mesh axis runs over, the one named last changes fastest.
Arguments:
- waveform: bfloat16 [2048, 512, 512], P('grp', 'seg')
- valid_count: int32 [2048, 512], P('grp', 'seg'), may hold values from 128 to 512
- plan: int32 [8, 8], replicated, may hold values from 0 to 7, as said below
Outputs:
- cross: bfloat16 [128, 2, 2048, 8, 256], P('seg', None, 'grp')
The draws below stay inside these ranges and needn't reach their ends.
Inputs may be any that keep to these rules, and one draw needn't show every extreme that they name: `plan`: row g lists, round by round, the partner group of group g: in every round g is the partner of its partner and each group is named once, and every row names each of the 8 groups at least once.
All inputs are finite; a program needn't handle non-finite values.
Results may differ from the reference program's by a relative error of at most 0.0061.
Values may be sent and summed in bfloat16 or wider, within the bound.
A program may use at most 128 MiB of HBM per device.

```python
import math
import jax
import jax.numpy as jnp
from jax import lax

SG = 256
F = 128
SAMPLES = 512
K0 = 2
NGROUPS = 8
ROUNDS = 8
STATIONS = 2048
SEGS = 512


def draw_waveform(key, part):
    key = jax.random.fold_in(key, 3)
    key_level, key_noise = jax.random.split(key, 2)
    level = jnp.exp(jax.random.uniform(key_level, (STATIONS, SEGS, 1), minval=0.0, maxval=math.log(10.0)))
    noise = jax.random.normal(key_noise, (STATIONS, SEGS, SAMPLES))
    return (level * noise).astype(jnp.float32).astype(jnp.bfloat16)


def draw_plan(key, part):
    key = jax.random.fold_in(key, 7)
    key_perm, key_more = jax.random.split(key, 2)
    first = jax.random.permutation(key_perm, NGROUPS).astype(jnp.int32)
    extra = jax.random.randint(key_more, (ROUNDS - NGROUPS,), 0, NGROUPS).astype(jnp.int32)
    masks = jnp.concatenate([first, extra], axis=0).astype(jnp.int32)
    groups = jnp.arange(NGROUPS, dtype=jnp.int32)
    return jnp.bitwise_xor(groups[:, None], masks[None, :]).astype(jnp.int32)


def set_ends(array, rng, smallest, top_value):
    extent = array.shape
    spot = [jax.random.randint(jax.random.fold_in(rng, axis), (), 0, extent[axis]) for axis in range(len(extent))]
    array = array.at[tuple(spot)].set(smallest)
    longest = extent.index(max(extent))
    spot[longest] = (spot[longest] + 1) % extent[longest]
    return array.at[tuple(spot)].set(top_value)


def setup_inputs(seed: int = 0) -> dict:
    key_list = jax.random.split(jax.random.key(seed), 4)
    return {
        "waveform": draw_waveform(jax.random.fold_in(key_list[3], 71), 0),
        "valid_count": set_ends(jax.random.randint(key_list[1], (STATIONS, SEGS), SAMPLES // 4, SAMPLES + 1), jax.random.fold_in(key_list[1], 1), SAMPLES // 4, SAMPLES).astype(jnp.int32),
        "plan": draw_plan(jax.random.fold_in(key_list[3], 71), 0),
    }


def make_basis(samples):
    times = jnp.arange(samples, dtype=jnp.int32)[:, None]
    bins = K0 + jnp.arange(F, dtype=jnp.int32)[None, :]
    phase = (times * bins % samples).astype(jnp.float32) * (2.0 * math.pi / samples)
    return jnp.concatenate([jnp.cos(phase), -jnp.sin(phase)], axis=1).astype(jnp.bfloat16)

def reference(waveform, valid_count, plan):
    basis = make_basis(SAMPLES)
    times = jnp.arange(SAMPLES, dtype=jnp.int32)
    gated = jnp.where(times[None, None, :] < valid_count[:, :, None], waveform, jnp.zeros_like(waveform))
    spectrum = jnp.dot(gated.reshape(STATIONS * SEGS, SAMPLES), basis, preferred_element_type=jnp.float32)
    spectrum = spectrum.reshape(STATIONS, SEGS, 2 * F)
    power = lax.optimization_barrier(jnp.sum(spectrum * spectrum, axis=-1)) / F
    keep = (valid_count >= SAMPLES // 2).astype(jnp.float32)
    weight = keep / jnp.sqrt(power + 1e-06)
    white = (spectrum * weight[:, :, None]).astype(jnp.bfloat16)
    owner = jnp.arange(STATIONS, dtype=jnp.int32) // SG
    columns = plan[owner][:, :, None] * SG + jnp.arange(SG, dtype=jnp.int32)[None, None, :]
    station_rows = jnp.arange(STATIONS, dtype=jnp.int32)[:, None, None]

    def one_bin(index):
        real_part = lax.dynamic_index_in_dim(white, index, 2, keepdims=False)
        imag_part = lax.dynamic_index_in_dim(white, index + F, 2, keepdims=False)
        cross_re = jnp.dot(real_part, real_part.T, preferred_element_type=jnp.float32) + jnp.dot(imag_part, imag_part.T, preferred_element_type=jnp.float32)
        cross_im = jnp.dot(imag_part, real_part.T, preferred_element_type=jnp.float32) - jnp.dot(real_part, imag_part.T, preferred_element_type=jnp.float32)
        full = jnp.stack([cross_re, cross_im], axis=0) / SEGS
        picked = full[:, station_rows, columns]
        return picked.astype(jnp.bfloat16)
    return lax.map(one_bin, jnp.arange(F, dtype=jnp.int32))
```

```python
import functools
import math

import jax
import jax.numpy as jnp
from jax import lax
from jax.experimental import pallas as pl
from jax.experimental.pallas import tpu as pltpu
from jax.sharding import PartitionSpec as P

F = 128
K0 = 2
MESH = pl.DeviceIdType.MESH

NY = 4
NZ = 2
NS = 32
PEERS = NZ * NS
BINS = 4
ROWS = 32
DEPTH = NS * ROWS
G = 256
NGRP = NZ * NY
TILE = 16


def make_basis(samples):
    times = jnp.arange(samples, dtype=jnp.int32)[:, None]
    bins = K0 + jnp.arange(F, dtype=jnp.int32)[None, :]
    phase = (times * bins % samples).astype(jnp.float32) * (2.0 * math.pi / samples)
    return jnp.concatenate([jnp.cos(phase), -jnp.sin(phase)], axis=1).astype(jnp.bfloat16)


def transpose_left(source, index, left):
    def step(c, carry):
        block = source[index, pl.ds(pl.multiple_of(c * 128, 128), 128), :]
        parts = block.reshape(8, 16, G)
        turned = []
        for m in range(4):
            turned += [parts[2 * m + 1], -parts[2 * m]]
        other = jnp.concatenate(turned, axis=0)
        at = pl.ds(pl.multiple_of(c * 128, 128), 128)
        left[pl.ds(0, G), at] = block.T
        left[pl.ds(G, G), at] = other.T
        return carry

    lax.fori_loop(0, DEPTH // 128, step, 0)


def product(left, right):
    full = jnp.dot(left[...], right, preferred_element_type=jnp.float32)
    return (full * (1.0 / 512.0)).astype(jnp.bfloat16)


def kernel(plan_ref, white, out, *scratch):
    spec = scratch[0:4]
    res = scratch[4:8]
    done = scratch[8:12]
    give, left, tmp = scratch[12:15]
    send1, recv1, send2, recv2, send3, recv3, out_sem = scratch[15:]
    g = lax.axis_index("grp")
    s = lax.axis_index("seg")
    zh, y = lax.div(g, NY), lax.rem(g, NY)
    me = zh * NS + s
    right = zh * NY + lax.rem(y + 1, NY)
    leftd = zh * NY + lax.rem(y + NY - 1, NY)

    def peer(d):
        p = lax.rem(me + d, PEERS)
        return lax.div(p, NS), lax.rem(p, NS)

    barrier = pltpu.get_barrier_semaphore()

    def greet(d, carry):
        pz, ps = peer(d)
        pl.semaphore_signal(barrier, inc=1, device_id=(pz * NY + y, ps), device_id_type=MESH)
        return carry

    lax.fori_loop(1, PEERS, greet, 0)
    for n in (right, leftd):
        pl.semaphore_signal(barrier, inc=1, device_id=(n, s), device_id_type=MESH)
    pl.semaphore_wait(barrier, PEERS + 1)

    mine = pl.ds(pl.multiple_of(s * ROWS, ROWS), ROWS)

    def scatter(b):
        def send(d, carry):
            pz, ps = peer(d)
            pltpu.make_async_remote_copy(
                src_ref=white.at[ps * BINS + b],
                dst_ref=spec[b].at[2 + zh, mine],
                send_sem=send1.at[b],
                recv_sem=recv1.at[b],
                device_id=(pz * NY + y, ps),
                device_id_type=MESH,
            ).start()
            return carry

        lax.fori_loop(1, PEERS, send, 0)
        pltpu.make_async_copy(white.at[s * BINS + b], spec[b].at[2 + zh, mine], recv1.at[b]).start()

    def scatter_arrived(b):
        own = spec[b].at[pl.ds(2, 2)]
        pltpu.make_async_copy(own, own, recv1.at[b]).wait()

    def scatter_left(b):
        some = white.at[pl.ds(0, PEERS - 1)]
        pltpu.make_async_copy(some, some, send1.at[b]).wait()

    def neighbour(b, side):
        to, at = ((right, 0), (leftd, 4))[side]
        return pltpu.make_async_remote_copy(
            src_ref=spec[b].at[pl.ds(2, 2)],
            dst_ref=spec[b].at[pl.ds(at, 2)],
            send_sem=send2.at[b, side],
            recv_sem=recv2.at[b, side],
            device_id=(to, s),
            device_id_type=MESH,
        )

    def gift(b, side):
        to, group = ((right, lax.rem(y + 3, NY)), (leftd, NY + lax.rem(y + 1, NY)))[side]
        return pltpu.make_async_remote_copy(
            src_ref=give.at[b, side],
            dst_ref=res[b].at[group],
            send_sem=send3.at[b, side],
            recv_sem=recv3.at[b, side],
            device_id=(to, s),
            device_id_type=MESH,
        )

    def multiply(b):
        transpose_left(spec[b], 4 + zh, left)
        give[b, 0] = product(left, spec[b][0])
        gift(b, 0).start()
        transpose_left(spec[b], zh, left)
        give[b, 1] = product(left, spec[b][5])
        gift(b, 1).start()
        transpose_left(spec[b], 2 + zh, left)

        def block(t, carry):
            group = lax.rem(t, 2) * NY + lax.rem(y + 3 + lax.div(t, 2), NY)
            res[b][group] = product(left, spec[b][t])
            return carry

        lax.fori_loop(0, 6, block, 0)

    def assemble(b):
        def tile(m, carry):
            rows = pl.ds(pl.multiple_of(m * TILE, TILE), TILE)
            for r in range(NGRP):
                piece = res[b][plan_ref[g, r], rows, :].astype(jnp.float32)
                for h in range(2):
                    tmp[h, pl.ds(r, TILE, NGRP), :] = piece[:, h * 128 : h * 128 + 128]
            at = pl.ds(pl.multiple_of(m * TILE * NGRP, TILE * NGRP), TILE * NGRP)
            for h in range(2):
                done[b][at, h * 128 : h * 128 + 128] = tmp[h].astype(jnp.bfloat16)
            return carry

        lax.fori_loop(0, 2 * G // TILE, tile, 0)
        pltpu.make_async_copy(done[b], out.at[b], out_sem.at[b]).start()

    scatter(0)
    scatter(1)
    for b in range(BINS + 1):
        if b < BINS:
            scatter_arrived(b)
            for side in range(2):
                neighbour(b, side).start()
            if b + 2 < BINS:
                scatter(b + 2)
        if b >= 1:
            for side in range(2):
                neighbour(b - 1, side).wait_recv()
            multiply(b - 1)
            if b >= 2:
                for side in range(2):
                    gift(b - 2, side).wait_recv()
                assemble(b - 2)
    for side in range(2):
        gift(BINS - 1, side).wait_recv()
    assemble(BINS - 1)
    for b in range(BINS):
        scatter_left(b)
        for side in range(2):
            neighbour(b, side).wait_send()
            gift(b, side).wait_send()
        pltpu.make_async_copy(done[b], out.at[b], out_sem.at[b]).wait()


def cross(plan, white):
    bf16 = jnp.bfloat16
    return pl.pallas_call(
        kernel,
        out_shape=jax.ShapeDtypeStruct((BINS, 2 * G * NGRP, G), bf16),
        in_specs=[
            pl.BlockSpec(memory_space=pltpu.SMEM),
            pl.BlockSpec(memory_space=pltpu.VMEM),
        ],
        out_specs=pl.BlockSpec(memory_space=pl.ANY),
        scratch_shapes=[pltpu.VMEM((6, DEPTH, G), bf16)] * BINS
        + [pltpu.VMEM((NGRP, 2 * G, G), bf16)] * BINS
        + [pltpu.VMEM((2 * G * NGRP, G), bf16)] * BINS
        + [
            pltpu.VMEM((BINS, 2, 2 * G, G), bf16),
            pltpu.VMEM((2 * G, DEPTH), bf16),
            pltpu.VMEM((2, TILE * NGRP, 128), jnp.float32),
            pltpu.SemaphoreType.DMA((BINS,)),
            pltpu.SemaphoreType.DMA((BINS,)),
            pltpu.SemaphoreType.DMA((BINS, 2)),
            pltpu.SemaphoreType.DMA((BINS, 2)),
            pltpu.SemaphoreType.DMA((BINS, 2)),
            pltpu.SemaphoreType.DMA((BINS, 2)),
            pltpu.SemaphoreType.DMA((BINS,)),
        ],
        compiler_params=pltpu.CompilerParams(
            collective_id=0, has_side_effects=True, vmem_limit_bytes=56 * 1024 * 1024
        ),
    )(plan, white)


def shards(waveform, valid_count, plan):
    group_rows, seg_local, samples = waveform.shape
    basis = make_basis(samples)
    times = lax.broadcasted_iota(jnp.int32, waveform.shape, 2)
    gated = jnp.where(times < valid_count[:, :, None], waveform, jnp.zeros_like(waveform))
    spectrum = jnp.einsum("tk,ist->ksi", basis, gated, preferred_element_type=jnp.float32)
    spectrum = spectrum.reshape(2, F, seg_local, group_rows)
    power = jnp.sum(spectrum * spectrum, axis=(0, 1)) / F
    keep = (valid_count.T >= samples // 2).astype(jnp.float32)
    weight = keep / jnp.sqrt(power + 1e-06)
    white = (spectrum * weight[None, None, :, :]).astype(jnp.bfloat16)
    white = white.transpose(1, 0, 2, 3).reshape(F, ROWS, G)
    return cross(plan, white).reshape(BINS, 2, G, NGRP, G)


def solution(mesh):
    return jax.shard_map(
        shards,
        mesh=mesh,
        in_specs=(P("grp", "seg", None), P("grp", "seg"), P()),
        out_specs=P("seg", None, "grp", None, None),
        check_vma=False,
    )
```

```python
import functools
import math

import jax
import jax.numpy as jnp
from jax import lax
from jax.experimental import pallas as pl
from jax.experimental.pallas import tpu as pltpu
from jax.sharding import PartitionSpec as P

F = 128
K0 = 2
MESH = pl.DeviceIdType.MESH

NY = 4
NZ = 2
NS = 32
PEERS = NZ * NS
BINS = 4
DEPTH = NS * 2 * 16
G = 256
NGRP = NZ * NY
TILE = 16
LAST = BINS - 1
AHEAD = 4
CUTS = [[(0, 0), (0, 128), (1, 0), (1, 128)]] * BINS


def make_basis(samples):
    times = jnp.arange(samples, dtype=jnp.int32)[:, None]
    bins = K0 + jnp.arange(F, dtype=jnp.int32)[None, :]
    phase = (times * bins % samples).astype(jnp.float32) * (2.0 * math.pi / samples)
    return jnp.concatenate([jnp.cos(phase), -jnp.sin(phase)], axis=1).astype(jnp.bfloat16)


def transpose_left(source, index, left):
    def step(c, carry):
        parts = source[index, pl.ds(c * 4, 4)]
        block = parts.reshape(128, G)
        turned = []
        for m in range(4):
            turned += [parts[m, 1], -parts[m, 0]]
        other = jnp.concatenate(turned, axis=0)
        at = pl.ds(pl.multiple_of(c * 128, 128), 128)
        left[pl.ds(0, G), at] = block.T
        left[pl.ds(G, G), at] = other.T
        return carry

    lax.fori_loop(0, DEPTH // 128, step, 0)


def product(left, right, index):
    full = jnp.dot(left[...], right[index].reshape(DEPTH, G), preferred_element_type=jnp.float32)
    return (full * (1.0 / 512.0)).astype(jnp.bfloat16)


def interleave(plan_ref, g, source, target, tmp, m):
    rows = pl.ds(pl.multiple_of(m * TILE, TILE), TILE)
    for r in range(NGRP):
        piece = source[plan_ref[g, r], rows, :].astype(jnp.float32)
        for h in range(2):
            tmp[h, pl.ds(r, TILE, NGRP), :] = piece[:, h * 128 : h * 128 + 128]
    at = pl.ds(pl.multiple_of(m * TILE * NGRP, TILE * NGRP), TILE * NGRP)
    for h in range(2):
        target[at, h * 128 : h * 128 + 128] = tmp[h].astype(jnp.bfloat16)


def kernel(plan_ref, white, mid, last, *scratch):
    spec = scratch[0:BINS]
    res = scratch[BINS : 2 * BINS - 1] + (last,)
    give, left, tmp = scratch[2 * BINS - 1 : 2 * BINS + 2]
    send1, recv1, send2, recv2, send3, recv3 = scratch[2 * BINS + 2 :]
    g = lax.axis_index("grp")
    s = lax.axis_index("seg")
    zh, y = lax.div(g, NY), lax.rem(g, NY)
    me = zh * NS + s
    right = zh * NY + lax.rem(y + 1, NY)
    leftd = zh * NY + lax.rem(y + NY - 1, NY)

    def peer(d):
        p = lax.rem(me + d, PEERS)
        return lax.div(p, NS), lax.rem(p, NS)

    barrier = pltpu.get_barrier_semaphore()

    def greet(d, carry):
        pz, ps = peer(d)
        pl.semaphore_signal(barrier, inc=1, device_id=(pz * NY + y, ps), device_id_type=MESH)
        return carry

    lax.fori_loop(1, PEERS, greet, 0)
    for n in (right, leftd):
        pl.semaphore_signal(barrier, inc=1, device_id=(n, s), device_id_type=MESH)
    pl.semaphore_wait(barrier, PEERS + 1)

    def cut(ref, where):
        part, lane = where
        lead = (slice(None),) * (len(ref.shape) - 3)
        if lane is None:
            return ref.at[lead + (part,)]
        return ref.at[lead + (part, slice(None), pl.ds(lane, 128))]

    def scatter(b, q):
        where = CUTS[b][q]

        def send(d, carry):
            pz, ps = peer(d)
            pltpu.make_async_remote_copy(
                src_ref=cut(white.at[ps * BINS + b], where),
                dst_ref=cut(spec[b].at[2 + zh, s], where),
                send_sem=send1.at[b, q],
                recv_sem=recv1.at[b, q],
                device_id=(pz * NY + y, ps),
                device_id_type=MESH,
            ).start()
            return carry

        lax.fori_loop(1, PEERS, send, 0)
        pltpu.make_async_copy(
            cut(white.at[s * BINS + b], where), cut(spec[b].at[2 + zh, s], where), recv1.at[b, q]
        ).start()

    def scatter_arrived(b, q):
        own = cut(spec[b].at[pl.ds(2, 2)], CUTS[b][q])
        pltpu.make_async_copy(own, own, recv1.at[b, q]).wait()

    def scatter_left(b, q):
        some = cut(white.at[pl.ds(0, PEERS - 1)], CUTS[b][q])
        pltpu.make_async_copy(some, some, send1.at[b, q]).wait()

    def neighbour(b, q, side):
        to, at = ((right, 0), (leftd, 4))[side]
        return pltpu.make_async_remote_copy(
            src_ref=cut(spec[b].at[pl.ds(2, 2)], CUTS[b][q]),
            dst_ref=cut(spec[b].at[pl.ds(at, 2)], CUTS[b][q]),
            send_sem=send2.at[b, q, side],
            recv_sem=recv2.at[b, q, side],
            device_id=(to, s),
            device_id_type=MESH,
        )

    def gift(b, side):
        to, group = ((right, lax.rem(y + 3, NY)), (leftd, NY + lax.rem(y + 1, NY)))[side]
        return pltpu.make_async_remote_copy(
            src_ref=give.at[b, side],
            dst_ref=res[b].at[group],
            send_sem=send3.at[b, side],
            recv_sem=recv3.at[b, side],
            device_id=(to, s),
            device_id_type=MESH,
        )

    def multiply(b):
        transpose_left(spec[b], 4 + zh, left)
        give[b, 0] = product(left, spec[b], 0)
        gift(b, 0).start()
        transpose_left(spec[b], zh, left)
        give[b, 1] = product(left, spec[b], 5)
        gift(b, 1).start()
        transpose_left(spec[b], 2 + zh, left)

        def block(t, carry):
            group = lax.rem(t, 2) * NY + lax.rem(y + 3 + lax.div(t, 2), NY)
            res[b][group] = product(left, spec[b], t)
            return carry

        lax.fori_loop(0, 6, block, 0)

    def assemble(b):
        def tile(m, carry):
            interleave(plan_ref, g, res[b], mid.at[b], tmp, m)
            return carry

        lax.fori_loop(0, 2 * G // TILE, tile, 0)

    def finish(b):
        for q in range(len(CUTS[b])):
            for side in range(2):
                neighbour(b, q, side).wait_recv()
        multiply(b)
        if b >= 1:
            for side in range(2):
                gift(b - 1, side).wait_recv()
            assemble(b - 1)

    steps = [(b, q) for b in range(BINS) for q in range(len(CUTS[b]))]
    ahead = AHEAD
    for b, q in steps[:ahead]:
        scatter(b, q)
    for k, (b, q) in enumerate(steps):
        scatter_arrived(b, q)
        for side in range(2):
            neighbour(b, q, side).start()
        while ahead < len(steps) and ahead <= k + AHEAD:
            scatter(*steps[ahead])
            ahead += 1
        if b >= 1 and q == 0:
            finish(b - 1)
    finish(LAST)
    for side in range(2):
        gift(LAST, side).wait_recv()
    for b, q in steps:
        scatter_left(b, q)
        for side in range(2):
            neighbour(b, q, side).wait_send()
    for b in range(BINS):
        for side in range(2):
            gift(b, side).wait_send()


def cross(plan, white):
    bf16 = jnp.bfloat16
    most = max(len(c) for c in CUTS)
    return pl.pallas_call(
        kernel,
        out_shape=(
            pltpu.VMEM((LAST, 2 * G * NGRP, G), bf16),
            pltpu.VMEM((NGRP, 2 * G, G), bf16),
        ),
        in_specs=[
            pl.BlockSpec(memory_space=pltpu.SMEM),
            pl.BlockSpec(memory_space=pltpu.VMEM),
        ],
        out_specs=(pl.BlockSpec(memory_space=pltpu.VMEM),) * 2,
        scratch_shapes=[pltpu.VMEM((6, NS, 2, TILE, G), bf16)] * BINS
        + [pltpu.VMEM((NGRP, 2 * G, G), bf16)] * LAST
        + [
            pltpu.VMEM((BINS, 2, 2 * G, G), bf16),
            pltpu.VMEM((2 * G, DEPTH), bf16),
            pltpu.VMEM((2, TILE * NGRP, 128), jnp.float32),
            pltpu.SemaphoreType.DMA((BINS, most)),
            pltpu.SemaphoreType.DMA((BINS, most)),
            pltpu.SemaphoreType.DMA((BINS, most, 2)),
            pltpu.SemaphoreType.DMA((BINS, most, 2)),
            pltpu.SemaphoreType.DMA((BINS, 2)),
            pltpu.SemaphoreType.DMA((BINS, 2)),
        ],
        compiler_params=pltpu.CompilerParams(
            collective_id=0, has_side_effects=True, vmem_limit_bytes=36 * 1024 * 1024
        ),
    )(plan, pltpu.with_memory_space_constraint(white, pltpu.VMEM))


QUARTERS = 4


def place_kernel(plan_ref, mid, last, out, target, tmp, mid_sem, out_sem):
    g = lax.axis_index("grp")

    def keep(b):
        return pltpu.make_async_copy(mid.at[b], out.at[b], mid_sem.at[b])

    for b in range(LAST):
        keep(b).start()
    size = 2 * G * NGRP // QUARTERS

    def store(q):
        rows = pl.ds(q * size, size)
        return pltpu.make_async_copy(target.at[rows], out.at[LAST, rows], out_sem.at[q])

    def tile(m, carry):
        interleave(plan_ref, g, last, target, tmp, m)
        return carry

    each = 2 * G // TILE // QUARTERS
    for q in range(QUARTERS):
        lax.fori_loop(q * each, (q + 1) * each, tile, 0)
        store(q).start()
    for q in range(QUARTERS):
        store(q).wait()
    for b in range(LAST):
        keep(b).wait()


def place(plan, mid, last):
    bf16 = jnp.bfloat16
    return pl.pallas_call(
        place_kernel,
        out_shape=jax.ShapeDtypeStruct((BINS, 2 * G * NGRP, G), bf16),
        in_specs=[
            pl.BlockSpec(memory_space=pltpu.SMEM),
            pl.BlockSpec(memory_space=pltpu.VMEM),
            pl.BlockSpec(memory_space=pltpu.VMEM),
        ],
        out_specs=pl.BlockSpec(memory_space=pl.ANY),
        scratch_shapes=[
            pltpu.VMEM((2 * G * NGRP, G), bf16),
            pltpu.VMEM((2, TILE * NGRP, 128), jnp.float32),
            pltpu.SemaphoreType.DMA((LAST,)),
            pltpu.SemaphoreType.DMA((QUARTERS,)),
        ],
        compiler_params=pltpu.CompilerParams(vmem_limit_bytes=16 * 1024 * 1024),
    )(
        plan,
        pltpu.with_memory_space_constraint(mid, pltpu.VMEM),
        pltpu.with_memory_space_constraint(last, pltpu.VMEM),
    )


def shards(waveform, valid_count, plan):
    group_rows, seg_local, samples = waveform.shape
    basis = make_basis(samples)
    times = lax.broadcasted_iota(jnp.int32, waveform.shape, 2)
    gated = jnp.where(times < valid_count[:, :, None], waveform, jnp.zeros_like(waveform))
    spectrum = jnp.einsum("tk,ist->ksi", basis, gated, preferred_element_type=jnp.float32)
    spectrum = spectrum.reshape(2, F, seg_local, group_rows)
    power = jnp.sum(spectrum * spectrum, axis=(0, 1)) / F
    keep = (valid_count.T >= samples // 2).astype(jnp.float32)
    weight = keep / jnp.sqrt(power + 1e-06)
    white = (spectrum * weight[None, None, :, :]).astype(jnp.bfloat16)
    white = white.transpose(1, 0, 2, 3)
    mid, last = cross(plan, white)
    return place(plan, mid, last).reshape(BINS, 2, G, NGRP, G)


def solution(mesh):
    return jax.shard_map(
        shards,
        mesh=mesh,
        in_specs=(P("grp", "seg", None), P("grp", "seg"), P()),
        out_specs=P("seg", None, "grp", None, None),
        check_vma=False,
    )
```

```python
import functools
import math

import jax
import jax.numpy as jnp
import numpy as np
from jax import lax
from jax.experimental import pallas as pl
from jax.experimental.pallas import tpu as pltpu
from jax.sharding import PartitionSpec as P

F = 128
K0 = 2
MESH = pl.DeviceIdType.MESH

NY = 4
NZ = 2
NS = 32
PEERS = NZ * NS
BINS = 4
DEPTH = NS * 2 * 16
G = 256
NGRP = NZ * NY
TILE = 16
LAST = BINS - 1
AHEAD = 4
CUTS = [[(0, 0), (0, 128), (1, 0), (1, 128)]] * BINS


def make_basis(samples):
    times = np.arange(samples, dtype=np.int32)[:, None]
    bins = K0 + np.arange(F, dtype=np.int32)[None, :]
    phase = (times * bins % samples).astype(np.float32) * np.float32(2.0 * math.pi / samples)
    return np.concatenate([np.cos(phase), -np.sin(phase)], axis=1).astype(jnp.bfloat16)


CHUNKS = 2


def whiten(wave, valid, basis, out, held, rows, turned, counts, sem):
    size = G // CHUNKS

    def load(c):
        return pltpu.make_async_copy(wave.at[pl.ds(c * size, size)], held.at[c], sem.at[c])

    for c in range(CHUNKS):
        load(c).start()
    samples = held.shape[-1]
    count = valid[...].T
    counts[...] = jnp.where(count >= samples // 2, count, 0)
    for c in range(CHUNKS):
        load(c).wait()
        limit = counts[pl.ds(c * size, size), :]
        times = lax.broadcasted_iota(jnp.int32, (size, TILE, samples), 2)
        gated = jnp.where(times < limit[:, :, None], held[c].astype(jnp.float32), 0.0)
        gated = gated.astype(jnp.bfloat16).reshape(size * TILE, samples)
        spectrum = jnp.dot(gated, basis[...], preferred_element_type=jnp.float32)
        power = jnp.sum(spectrum * spectrum, axis=1, keepdims=True) * (1.0 / F)
        spectrum = spectrum * lax.rsqrt(power + 1e-06)
        for h in range(2):
            rows[h] = spectrum[:, h * 128 : h * 128 + 128]
        for k in range(TILE):
            for h in range(2):
                turned[h, pl.ds(k, F, TILE), :] = rows[h, pl.ds(k, size, TILE), :].T
        for h in range(2):
            block = turned[h].reshape(F, TILE, size).astype(jnp.bfloat16)
            out[:, h, :, c * size : c * size + size] = block


def transpose_left(source, index, left):
    def step(c, carry):
        parts = source[index, pl.ds(c * 4, 4)]
        block = parts.reshape(128, G)
        turned = []
        for m in range(4):
            turned += [parts[m, 1], -parts[m, 0]]
        other = jnp.concatenate(turned, axis=0)
        at = pl.ds(pl.multiple_of(c * 128, 128), 128)
        left[pl.ds(0, G), at] = block.T
        left[pl.ds(G, G), at] = other.T
        return carry

    lax.fori_loop(0, DEPTH // 128, step, 0)


def product(left, right, index):
    full = jnp.dot(left[...], right[index].reshape(DEPTH, G), preferred_element_type=jnp.float32)
    return (full * (1.0 / 512.0)).astype(jnp.bfloat16)


def interleave(plan_ref, g, source, target, tmp, m):
    rows = pl.ds(pl.multiple_of(m * TILE, TILE), TILE)
    for r in range(NGRP):
        piece = source[plan_ref[g, r], rows, :].astype(jnp.float32)
        for h in range(2):
            tmp[h, pl.ds(r, TILE, NGRP), :] = piece[:, h * 128 : h * 128 + 128]
    at = pl.ds(pl.multiple_of(m * TILE * NGRP, TILE * NGRP), TILE * NGRP)
    for h in range(2):
        target[at, h * 128 : h * 128 + 128] = tmp[h].astype(jnp.bfloat16)


def kernel(plan_ref, wave, valid, basis, mid, last, *scratch):
    spec = scratch[0:BINS]
    res = scratch[BINS : 2 * BINS - 1] + (last,)
    give, left, tmp = scratch[2 * BINS - 1 : 2 * BINS + 2]
    send1, recv1, send2, recv2, send3, recv3 = scratch[2 * BINS + 2 : -6]
    white = scratch[-6]
    g = lax.axis_index("grp")
    s = lax.axis_index("seg")
    zh, y = lax.div(g, NY), lax.rem(g, NY)
    me = zh * NS + s
    right = zh * NY + lax.rem(y + 1, NY)
    leftd = zh * NY + lax.rem(y + NY - 1, NY)

    def peer(d):
        p = lax.rem(me + d, PEERS)
        return lax.div(p, NS), lax.rem(p, NS)

    barrier = pltpu.get_barrier_semaphore()

    def greet(d, carry):
        pz, ps = peer(d)
        pl.semaphore_signal(barrier, inc=1, device_id=(pz * NY + y, ps), device_id_type=MESH)
        return carry

    lax.fori_loop(1, PEERS, greet, 0, unroll=7)
    for n in (right, leftd):
        pl.semaphore_signal(barrier, inc=1, device_id=(n, s), device_id_type=MESH)
    whiten(wave, valid, basis, *scratch[-6:])
    pl.semaphore_wait(barrier, PEERS + 1)

    def cut(ref, where):
        part, lane = where
        lead = (slice(None),) * (len(ref.shape) - 3)
        if lane is None:
            return ref.at[lead + (part,)]
        return ref.at[lead + (part, slice(None), pl.ds(lane, 128))]

    def scatter(b, q):
        where = CUTS[b][q]

        def send(d, carry):
            pz, ps = peer(d)
            pltpu.make_async_remote_copy(
                src_ref=cut(white.at[ps * BINS + b], where),
                dst_ref=cut(spec[b].at[2 + zh, s], where),
                send_sem=send1.at[b, q],
                recv_sem=recv1.at[b, q],
                device_id=(pz * NY + y, ps),
                device_id_type=MESH,
            ).start()
            return carry

        lax.fori_loop(1, PEERS, send, 0, unroll=7)
        pltpu.make_async_copy(
            cut(white.at[s * BINS + b], where), cut(spec[b].at[2 + zh, s], where), recv1.at[b, q]
        ).start()

    def scatter_arrived(b, q):
        own = cut(spec[b].at[pl.ds(2, 2)], CUTS[b][q])
        pltpu.make_async_copy(own, own, recv1.at[b, q]).wait()

    def scatter_left(b, q):
        some = cut(white.at[pl.ds(0, PEERS - 1)], CUTS[b][q])
        pltpu.make_async_copy(some, some, send1.at[b, q]).wait()

    def neighbour(b, q, side):
        to, at = ((right, 0), (leftd, 4))[side]
        return pltpu.make_async_remote_copy(
            src_ref=cut(spec[b].at[pl.ds(2, 2)], CUTS[b][q]),
            dst_ref=cut(spec[b].at[pl.ds(at, 2)], CUTS[b][q]),
            send_sem=send2.at[b, q, side],
            recv_sem=recv2.at[b, q, side],
            device_id=(to, s),
            device_id_type=MESH,
        )

    def gift(b, side):
        to, group = ((right, lax.rem(y + 3, NY)), (leftd, NY + lax.rem(y + 1, NY)))[side]
        return pltpu.make_async_remote_copy(
            src_ref=give.at[b, side],
            dst_ref=res[b].at[group],
            send_sem=send3.at[b, side],
            recv_sem=recv3.at[b, side],
            device_id=(to, s),
            device_id_type=MESH,
        )

    def multiply(b):
        transpose_left(spec[b], 4 + zh, left)
        give[b, 0] = product(left, spec[b], 0)
        gift(b, 0).start()
        transpose_left(spec[b], zh, left)
        give[b, 1] = product(left, spec[b], 5)
        gift(b, 1).start()
        transpose_left(spec[b], 2 + zh, left)

        def block(t, carry):
            group = lax.rem(t, 2) * NY + lax.rem(y + 3 + lax.div(t, 2), NY)
            res[b][group] = product(left, spec[b], t)
            return carry

        lax.fori_loop(0, 6, block, 0)

    def assemble(b):
        def tile(m, carry):
            interleave(plan_ref, g, res[b], mid.at[b], tmp, m)
            return carry

        lax.fori_loop(0, 2 * G // TILE, tile, 0)

    def finish(b):
        for q in range(len(CUTS[b])):
            for side in range(2):
                neighbour(b, q, side).wait_recv()
        multiply(b)
        if b >= 1:
            for side in range(2):
                gift(b - 1, side).wait_recv()
            assemble(b - 1)

    steps = [(b, q) for b in range(BINS) for q in range(len(CUTS[b]))]
    ahead = AHEAD
    for b, q in steps[:ahead]:
        scatter(b, q)
    for k, (b, q) in enumerate(steps):
        scatter_arrived(b, q)
        for side in range(2):
            neighbour(b, q, side).start()
        while ahead < len(steps) and ahead <= k + AHEAD:
            scatter(*steps[ahead])
            ahead += 1
        if b >= 1 and q == 0:
            finish(b - 1)
    finish(LAST)
    for side in range(2):
        gift(LAST, side).wait_recv()
    for b, q in steps:
        scatter_left(b, q)
        for side in range(2):
            neighbour(b, q, side).wait_send()
    for b in range(BINS):
        for side in range(2):
            gift(b, side).wait_send()


def cross(plan, waveform, valid_count):
    bf16 = jnp.bfloat16
    samples = waveform.shape[-1]
    most = max(len(c) for c in CUTS)
    return pl.pallas_call(
        kernel,
        out_shape=(
            pltpu.VMEM((LAST, 2 * G * NGRP, G), bf16),
            pltpu.VMEM((NGRP, 2 * G, G), bf16),
        ),
        in_specs=[
            pl.BlockSpec(memory_space=pltpu.SMEM),
            pl.BlockSpec(memory_space=pl.ANY),
            pl.BlockSpec(memory_space=pltpu.VMEM),
            pl.BlockSpec(memory_space=pltpu.VMEM),
        ],
        out_specs=(pl.BlockSpec(memory_space=pltpu.VMEM),) * 2,
        scratch_shapes=[pltpu.VMEM((6, NS, 2, TILE, G), bf16)] * BINS
        + [pltpu.VMEM((NGRP, 2 * G, G), bf16)] * LAST
        + [
            pltpu.VMEM((BINS, 2, 2 * G, G), bf16),
            pltpu.VMEM((2 * G, DEPTH), bf16),
            pltpu.VMEM((2, TILE * NGRP, 128), jnp.float32),
            pltpu.SemaphoreType.DMA((BINS, most)),
            pltpu.SemaphoreType.DMA((BINS, most)),
            pltpu.SemaphoreType.DMA((BINS, most, 2)),
            pltpu.SemaphoreType.DMA((BINS, most, 2)),
            pltpu.SemaphoreType.DMA((BINS, 2)),
            pltpu.SemaphoreType.DMA((BINS, 2)),
            pltpu.VMEM((F, 2, TILE, G), bf16),
            pltpu.VMEM((CHUNKS, G // CHUNKS, TILE, samples), bf16),
            pltpu.VMEM((2, G // CHUNKS * TILE, 128), jnp.float32),
            pltpu.VMEM((2, F * TILE, G // CHUNKS), jnp.float32),
            pltpu.VMEM((G, TILE), jnp.int32),
            pltpu.SemaphoreType.DMA((CHUNKS,)),
        ],
        compiler_params=pltpu.CompilerParams(
            collective_id=0, has_side_effects=True, vmem_limit_bytes=52 * 1024 * 1024
        ),
    )(plan, waveform, valid_count.T, make_basis(samples))


QUARTERS = 4


def place_kernel(plan_ref, mid, last, out, target, tmp, mid_sem, out_sem):
    g = lax.axis_index("grp")

    def keep(b):
        return pltpu.make_async_copy(mid.at[b], out.at[b], mid_sem.at[b])

    for b in range(LAST):
        keep(b).start()
    size = 2 * G * NGRP // QUARTERS

    def store(q):
        rows = pl.ds(q * size, size)
        return pltpu.make_async_copy(target.at[rows], out.at[LAST, rows], out_sem.at[q])

    def tile(m, carry):
        interleave(plan_ref, g, last, target, tmp, m)
        return carry

    each = 2 * G // TILE // QUARTERS
    for q in range(QUARTERS):
        lax.fori_loop(q * each, (q + 1) * each, tile, 0)
        store(q).start()
    for q in range(QUARTERS):
        store(q).wait()
    for b in range(LAST):
        keep(b).wait()


def place(plan, mid, last):
    bf16 = jnp.bfloat16
    return pl.pallas_call(
        place_kernel,
        out_shape=jax.ShapeDtypeStruct((BINS, 2 * G * NGRP, G), bf16),
        in_specs=[
            pl.BlockSpec(memory_space=pltpu.SMEM),
            pl.BlockSpec(memory_space=pltpu.VMEM),
            pl.BlockSpec(memory_space=pltpu.VMEM),
        ],
        out_specs=pl.BlockSpec(memory_space=pl.ANY),
        scratch_shapes=[
            pltpu.VMEM((2 * G * NGRP, G), bf16),
            pltpu.VMEM((2, TILE * NGRP, 128), jnp.float32),
            pltpu.SemaphoreType.DMA((LAST,)),
            pltpu.SemaphoreType.DMA((QUARTERS,)),
        ],
        compiler_params=pltpu.CompilerParams(vmem_limit_bytes=16 * 1024 * 1024),
    )(
        plan,
        pltpu.with_memory_space_constraint(mid, pltpu.VMEM),
        pltpu.with_memory_space_constraint(last, pltpu.VMEM),
    )


def shards(waveform, valid_count, plan):
    mid, last = cross(plan, waveform, valid_count)
    return place(plan, mid, last).reshape(BINS, 2, G, NGRP, G)


def solution(mesh):
    return jax.shard_map(
        shards,
        mesh=mesh,
        in_specs=(P("grp", "seg", None), P("grp", "seg"), P()),
        out_specs=P("seg", None, "grp", None, None),
        check_vma=False,
    )
```

```python
import functools
import math

import jax
import jax.numpy as jnp
import numpy as np
from jax import lax
from jax.experimental import pallas as pl
from jax.experimental.pallas import tpu as pltpu
from jax.sharding import PartitionSpec as P

F = 128
K0 = 2
MESH = pl.DeviceIdType.MESH

NY = 4
NZ = 2
NS = 32
PEERS = NZ * NS
BINS = 4
DEPTH = NS * 2 * 16
G = 256
NGRP = NZ * NY
TILE = 16
LAST = BINS - 1
AHEAD = 4
CUTS = [[(0, 0), (0, 128), (1, 0), (1, 128)]] * BINS


def make_basis(samples):
    times = np.arange(samples, dtype=np.int32)[:, None]
    bins = K0 + np.arange(F, dtype=np.int32)[None, :]
    phase = (times * bins % samples).astype(np.float32) * np.float32(2.0 * math.pi / samples)
    return np.concatenate([np.cos(phase), -np.sin(phase)], axis=1).astype(jnp.bfloat16)


CHUNKS = 2


PIECE = 128


def load_wave(wave, held, sem, n):
    some = pl.ds(pl.multiple_of(n * PIECE, PIECE), PIECE)
    return pltpu.make_async_copy(wave.at[some], held.at[some], sem.at[n])


def whiten(wave, valid, basis, out, held, rows, turned, counts, sem):
    size = G // CHUNKS
    samples = held.shape[-1]
    count = valid[...].T
    counts[...] = jnp.where(count >= samples // 2, count, 0)

    for c in range(CHUNKS):
        def piece(m, carry):
            n = c * (size // PIECE) + m
            load_wave(wave, held, sem, n).wait()
            some = pl.ds(pl.multiple_of(n * PIECE, PIECE), PIECE)
            limit = counts[some, :]
            times = lax.broadcasted_iota(jnp.int32, (PIECE, TILE, samples), 2)
            gated = jnp.where(times < limit[:, :, None], held[some].astype(jnp.float32), 0.0)
            gated = gated.astype(jnp.bfloat16).reshape(PIECE * TILE, samples)
            spectrum = jnp.dot(gated, basis[...], preferred_element_type=jnp.float32)
            power = jnp.sum(spectrum * spectrum, axis=1, keepdims=True) * (1.0 / F)
            spectrum = spectrum * lax.rsqrt(power + 1e-06)
            at = pl.ds(pl.multiple_of(m * PIECE * TILE, PIECE * TILE), PIECE * TILE)
            for h in range(2):
                rows[h, at, :] = spectrum[:, h * 128 : h * 128 + 128]
            return carry

        lax.fori_loop(0, size // PIECE, piece, 0)
        for k in range(TILE):
            for h in range(2):
                turned[h, pl.ds(k, F, TILE), :] = rows[h, pl.ds(k, size, TILE), :].T
        for h in range(2):
            block = turned[h].reshape(F, TILE, size).astype(jnp.bfloat16)
            out[:, h, :, c * size : c * size + size] = block


def transpose_left(source, index, left):
    def step(c, carry):
        parts = source[index, pl.ds(c * 4, 4)]
        block = parts.reshape(128, G)
        turned = []
        for m in range(4):
            turned += [parts[m, 1], -parts[m, 0]]
        other = jnp.concatenate(turned, axis=0)
        at = pl.ds(pl.multiple_of(c * 128, 128), 128)
        left[pl.ds(0, G), at] = block.T
        left[pl.ds(G, G), at] = other.T
        return carry

    lax.fori_loop(0, DEPTH // 128, step, 0)


def product(left, right, index):
    full = jnp.dot(left[...], right[index].reshape(DEPTH, G), preferred_element_type=jnp.float32)
    return (full * (1.0 / 512.0)).astype(jnp.bfloat16)


def interleave(plan_ref, g, source, target, tmp, m):
    rows = pl.ds(pl.multiple_of(m * TILE, TILE), TILE)
    for r in range(NGRP):
        piece = source[plan_ref[g, r], rows, :].astype(jnp.float32)
        for h in range(2):
            tmp[h, pl.ds(r, TILE, NGRP), :] = piece[:, h * 128 : h * 128 + 128]
    at = pl.ds(pl.multiple_of(m * TILE * NGRP, TILE * NGRP), TILE * NGRP)
    for h in range(2):
        target[at, h * 128 : h * 128 + 128] = tmp[h].astype(jnp.bfloat16)


def kernel(plan_ref, wave, valid, basis, mid, last, *scratch):
    spec = scratch[0:BINS]
    res = scratch[BINS : 2 * BINS - 1] + (last,)
    give, left, tmp = scratch[2 * BINS - 1 : 2 * BINS + 2]
    send1, recv1, send2, recv2, send3, recv3 = scratch[2 * BINS + 2 : -6]
    white, held = scratch[-6], scratch[-5]
    wave_sem = scratch[-1]
    for n in range(G // PIECE):
        load_wave(wave, held, wave_sem, n).start()
    g = lax.axis_index("grp")
    s = lax.axis_index("seg")
    zh, y = lax.div(g, NY), lax.rem(g, NY)
    me = zh * NS + s
    right = zh * NY + lax.rem(y + 1, NY)
    leftd = zh * NY + lax.rem(y + NY - 1, NY)

    def peer(d):
        p = lax.rem(me + d, PEERS)
        return lax.div(p, NS), lax.rem(p, NS)

    barrier = pltpu.get_barrier_semaphore()

    def greet(d, carry):
        pz, ps = peer(d)
        pl.semaphore_signal(barrier, inc=1, device_id=(pz * NY + y, ps), device_id_type=MESH)
        return carry

    lax.fori_loop(1, PEERS, greet, 0, unroll=7)
    for n in (right, leftd):
        pl.semaphore_signal(barrier, inc=1, device_id=(n, s), device_id_type=MESH)
    whiten(wave, valid, basis, *scratch[-6:])
    pl.semaphore_wait(barrier, PEERS + 1)

    def cut(ref, where):
        part, lane = where
        lead = (slice(None),) * (len(ref.shape) - 3)
        if lane is None:
            return ref.at[lead + (part,)]
        return ref.at[lead + (part, slice(None), pl.ds(lane, 128))]

    def scatter(b, q):
        where = CUTS[b][q]

        def send(d, carry):
            pz, ps = peer(d)
            pltpu.make_async_remote_copy(
                src_ref=cut(white.at[ps * BINS + b], where),
                dst_ref=cut(spec[b].at[2 + zh, s], where),
                send_sem=send1.at[b, q],
                recv_sem=recv1.at[b, q],
                device_id=(pz * NY + y, ps),
                device_id_type=MESH,
            ).start()
            return carry

        lax.fori_loop(1, PEERS, send, 0, unroll=7)
        pltpu.make_async_copy(
            cut(white.at[s * BINS + b], where), cut(spec[b].at[2 + zh, s], where), recv1.at[b, q]
        ).start()

    def scatter_arrived(b, q):
        own = cut(spec[b].at[pl.ds(2, 2)], CUTS[b][q])
        pltpu.make_async_copy(own, own, recv1.at[b, q]).wait()

    def scatter_left(b, q):
        some = cut(white.at[pl.ds(0, PEERS - 1)], CUTS[b][q])
        pltpu.make_async_copy(some, some, send1.at[b, q]).wait()

    def neighbour(b, q, side):
        to, at = ((right, 0), (leftd, 4))[side]
        return pltpu.make_async_remote_copy(
            src_ref=cut(spec[b].at[pl.ds(2, 2)], CUTS[b][q]),
            dst_ref=cut(spec[b].at[pl.ds(at, 2)], CUTS[b][q]),
            send_sem=send2.at[b, q, side],
            recv_sem=recv2.at[b, q, side],
            device_id=(to, s),
            device_id_type=MESH,
        )

    def gift(b, side):
        to, group = ((right, lax.rem(y + 3, NY)), (leftd, NY + lax.rem(y + 1, NY)))[side]
        return pltpu.make_async_remote_copy(
            src_ref=give.at[b, side],
            dst_ref=res[b].at[group],
            send_sem=send3.at[b, side],
            recv_sem=recv3.at[b, side],
            device_id=(to, s),
            device_id_type=MESH,
        )

    def multiply(b):
        transpose_left(spec[b], 4 + zh, left)
        give[b, 0] = product(left, spec[b], 0)
        gift(b, 0).start()
        transpose_left(spec[b], zh, left)
        give[b, 1] = product(left, spec[b], 5)
        gift(b, 1).start()
        transpose_left(spec[b], 2 + zh, left)

        def block(t, carry):
            group = lax.rem(t, 2) * NY + lax.rem(y + 3 + lax.div(t, 2), NY)
            res[b][group] = product(left, spec[b], t)
            return carry

        lax.fori_loop(0, 6, block, 0)

    def assemble(b):
        def tile(m, carry):
            interleave(plan_ref, g, res[b], mid.at[b], tmp, m)
            return carry

        lax.fori_loop(0, 2 * G // TILE, tile, 0)

    def finish(b):
        for q in range(len(CUTS[b])):
            for side in range(2):
                neighbour(b, q, side).wait_recv()
        multiply(b)
        if b >= 1:
            for side in range(2):
                gift(b - 1, side).wait_recv()
            assemble(b - 1)

    steps = [(b, q) for b in range(BINS) for q in range(len(CUTS[b]))]
    ahead = AHEAD
    for b, q in steps[:ahead]:
        scatter(b, q)
    for k, (b, q) in enumerate(steps):
        scatter_arrived(b, q)
        for side in range(2):
            neighbour(b, q, side).start()
        while ahead < len(steps) and ahead <= k + AHEAD:
            scatter(*steps[ahead])
            ahead += 1
        if b >= 1 and q == 0:
            finish(b - 1)
    finish(LAST)
    for side in range(2):
        gift(LAST, side).wait_recv()
    for b, q in steps:
        scatter_left(b, q)
        for side in range(2):
            neighbour(b, q, side).wait_send()
    for b in range(BINS):
        for side in range(2):
            gift(b, side).wait_send()


def cross(plan, waveform, valid_count):
    bf16 = jnp.bfloat16
    samples = waveform.shape[-1]
    most = max(len(c) for c in CUTS)
    return pl.pallas_call(
        kernel,
        out_shape=(
            pltpu.VMEM((LAST, 2 * G * NGRP, G), bf16),
            pltpu.VMEM((NGRP, 2 * G, G), bf16),
        ),
        in_specs=[
            pl.BlockSpec(memory_space=pltpu.SMEM),
            pl.BlockSpec(memory_space=pl.ANY),
            pl.BlockSpec(memory_space=pltpu.VMEM),
            pl.BlockSpec(memory_space=pltpu.VMEM),
        ],
        out_specs=(pl.BlockSpec(memory_space=pltpu.VMEM),) * 2,
        scratch_shapes=[pltpu.VMEM((6, NS, 2, TILE, G), bf16)] * BINS
        + [pltpu.VMEM((NGRP, 2 * G, G), bf16)] * LAST
        + [
            pltpu.VMEM((BINS, 2, 2 * G, G), bf16),
            pltpu.VMEM((2 * G, DEPTH), bf16),
            pltpu.VMEM((2, TILE * NGRP, 128), jnp.float32),
            pltpu.SemaphoreType.DMA((BINS, most)),
            pltpu.SemaphoreType.DMA((BINS, most)),
            pltpu.SemaphoreType.DMA((BINS, most, 2)),
            pltpu.SemaphoreType.DMA((BINS, most, 2)),
            pltpu.SemaphoreType.DMA((BINS, 2)),
            pltpu.SemaphoreType.DMA((BINS, 2)),
            pltpu.VMEM((F, 2, TILE, G), bf16),
            pltpu.VMEM((G, TILE, samples), bf16),
            pltpu.VMEM((2, G // CHUNKS * TILE, 128), jnp.float32),
            pltpu.VMEM((2, F * TILE, G // CHUNKS), jnp.float32),
            pltpu.VMEM((G, TILE), jnp.int32),
            pltpu.SemaphoreType.DMA((G // PIECE,)),
        ],
        compiler_params=pltpu.CompilerParams(
            collective_id=0, has_side_effects=True, vmem_limit_bytes=52 * 1024 * 1024
        ),
    )(plan, waveform, valid_count.T, make_basis(samples))


QUARTERS = 4


def place_kernel(plan, mid, last, out, plan_ref, target, tmp, plan_sem, mid_sem, out_sem):
    g = lax.axis_index("grp")

    def keep(b):
        return pltpu.make_async_copy(mid.at[b], out.at[b], mid_sem.at[b])

    fetch = pltpu.make_async_copy(plan, plan_ref, plan_sem)
    fetch.start()
    for b in range(LAST):
        keep(b).start()
    fetch.wait()
    size = 2 * G * NGRP // QUARTERS

    def store(q):
        rows = pl.ds(q * size, size)
        return pltpu.make_async_copy(target.at[rows], out.at[LAST, rows], out_sem.at[q])

    def tile(m, carry):
        interleave(plan_ref, g, last, target, tmp, m)
        return carry

    each = 2 * G // TILE // QUARTERS
    for q in range(QUARTERS):
        lax.fori_loop(q * each, (q + 1) * each, tile, 0)
        store(q).start()
    for q in range(QUARTERS):
        store(q).wait()
    for b in range(LAST):
        keep(b).wait()


def place(plan, mid, last):
    bf16 = jnp.bfloat16
    return pl.pallas_call(
        place_kernel,
        out_shape=jax.ShapeDtypeStruct((BINS, 2 * G * NGRP, G), bf16),
        in_specs=[
            pl.BlockSpec(memory_space=pltpu.HBM),
            pl.BlockSpec(memory_space=pltpu.VMEM),
            pl.BlockSpec(memory_space=pltpu.VMEM),
        ],
        out_specs=pl.BlockSpec(memory_space=pl.ANY),
        scratch_shapes=[
            pltpu.SMEM((NGRP, plan.shape[1]), jnp.int32),
            pltpu.VMEM((2 * G * NGRP, G), bf16),
            pltpu.VMEM((2, TILE * NGRP, 128), jnp.float32),
            pltpu.SemaphoreType.DMA,
            pltpu.SemaphoreType.DMA((LAST,)),
            pltpu.SemaphoreType.DMA((QUARTERS,)),
        ],
        compiler_params=pltpu.CompilerParams(vmem_limit_bytes=16 * 1024 * 1024),
    )(
        pltpu.with_memory_space_constraint(plan, pltpu.HBM),
        pltpu.with_memory_space_constraint(mid, pltpu.VMEM),
        pltpu.with_memory_space_constraint(last, pltpu.VMEM),
    )


def shards(waveform, valid_count, plan):
    mid, last = cross(plan, waveform, valid_count)
    return place(plan, mid, last).reshape(BINS, 2, G, NGRP, G)


def solution(mesh):
    return jax.shard_map(
        shards,
        mesh=mesh,
        in_specs=(P("grp", "seg", None), P("grp", "seg"), P()),
        out_specs=P("seg", None, "grp", None, None),
        check_vma=False,
    )
```

```python
import functools
import math

import jax
import jax.numpy as jnp
import numpy as np
from jax import lax
from jax.experimental import pallas as pl
from jax.experimental.pallas import tpu as pltpu
from jax.sharding import PartitionSpec as P

F = 128
K0 = 2
MESH = pl.DeviceIdType.MESH

NY = 4
NZ = 2
NS = 32
PEERS = NZ * NS
BINS = 4
DEPTH = NS * 2 * 16
G = 256
NGRP = NZ * NY
TILE = 16
LAST = BINS - 1
AHEAD = 4
CUTS = [[(0, 0), (0, 128), (1, 0), (1, 128)]] * BINS


def make_basis(samples):
    times = np.arange(samples, dtype=np.int32)[:, None]
    bins = K0 + np.arange(F, dtype=np.int32)[None, :]
    phase = (times * bins % samples).astype(np.float32) * np.float32(2.0 * math.pi / samples)
    return np.concatenate([np.cos(phase), -np.sin(phase)], axis=1).astype(jnp.bfloat16)


CHUNKS = 2


PIECE = 128


def load_wave(wave, held, sem, n):
    some = pl.ds(pl.multiple_of(n * PIECE, PIECE), PIECE)
    return pltpu.make_async_copy(wave.at[some], held.at[some], sem.at[n])


def whiten(wave, valid, basis, out, held, rows, turned, counts, sem):
    size = G // CHUNKS
    samples = held.shape[-1]
    count = valid[...].T
    counts[...] = jnp.where(count >= samples // 2, count, 0)

    for c in range(CHUNKS):
        def piece(m, carry):
            n = c * (size // PIECE) + m
            load_wave(wave, held, sem, n).wait()
            some = pl.ds(pl.multiple_of(n * PIECE, PIECE), PIECE)
            limit = counts[some, :]
            times = lax.broadcasted_iota(jnp.int32, (PIECE, TILE, samples), 2)
            gated = jnp.where(times < limit[:, :, None], held[some].astype(jnp.float32), 0.0)
            gated = gated.astype(jnp.bfloat16).reshape(PIECE * TILE, samples)
            spectrum = jnp.dot(gated, basis[...], preferred_element_type=jnp.float32)
            power = jnp.sum(spectrum * spectrum, axis=1, keepdims=True) * (1.0 / F)
            spectrum = spectrum * lax.rsqrt(power + 1e-06)
            at = pl.ds(pl.multiple_of(m * PIECE * TILE, PIECE * TILE), PIECE * TILE)
            for h in range(2):
                rows[h, at, :] = spectrum[:, h * 128 : h * 128 + 128]
            return carry

        lax.fori_loop(0, size // PIECE, piece, 0)
        for k in range(TILE):
            for h in range(2):
                turned[h, pl.ds(k, F, TILE), :] = rows[h, pl.ds(k, size, TILE), :].T
        for h in range(2):
            block = turned[h].reshape(F, TILE, size).astype(jnp.bfloat16)
            out[:, h, :, c * size : c * size + size] = block


def transpose_left(source, index, left):
    def step(c, carry):
        parts = source[index, pl.ds(c * 4, 4)]
        block = parts.reshape(128, G)
        turned = []
        for m in range(4):
            turned += [parts[m, 1], -parts[m, 0]]
        other = jnp.concatenate(turned, axis=0)
        at = pl.ds(pl.multiple_of(c * 128, 128), 128)
        left[pl.ds(0, G), at] = block.T
        left[pl.ds(G, G), at] = other.T
        return carry

    lax.fori_loop(0, DEPTH // 128, step, 0, unroll=4)


def product(left, right, index):
    full = jnp.dot(left[...], right[index].reshape(DEPTH, G), preferred_element_type=jnp.float32)
    return (full * (1.0 / 512.0)).astype(jnp.bfloat16)


def interleave(plan_ref, g, source, target, tmp, m):
    rows = pl.ds(pl.multiple_of(m * TILE, TILE), TILE)
    for r in range(NGRP):
        piece = source[plan_ref[g, r], rows, :].astype(jnp.float32)
        for h in range(2):
            tmp[h, pl.ds(r, TILE, NGRP), :] = piece[:, h * 128 : h * 128 + 128]
    at = pl.ds(pl.multiple_of(m * TILE * NGRP, TILE * NGRP), TILE * NGRP)
    for h in range(2):
        target[at, h * 128 : h * 128 + 128] = tmp[h].astype(jnp.bfloat16)


def kernel(plan_ref, wave, valid, basis, mid, last, *scratch):
    spec = scratch[0:BINS]
    res = scratch[BINS : 2 * BINS - 1] + (last,)
    give, left, tmp = scratch[2 * BINS - 1 : 2 * BINS + 2]
    send1, recv1, send2, recv2, send3, recv3 = scratch[2 * BINS + 2 : -6]
    white, held = scratch[-6], scratch[-5]
    wave_sem = scratch[-1]
    for n in range(G // PIECE):
        load_wave(wave, held, wave_sem, n).start()
    g = lax.axis_index("grp")
    s = lax.axis_index("seg")
    zh, y = lax.div(g, NY), lax.rem(g, NY)
    me = zh * NS + s
    right = zh * NY + lax.rem(y + 1, NY)
    leftd = zh * NY + lax.rem(y + NY - 1, NY)

    def peer(d):
        p = lax.rem(me + d, PEERS)
        return lax.div(p, NS), lax.rem(p, NS)

    barrier = pltpu.get_barrier_semaphore()

    def greet(d, carry):
        pz, ps = peer(d)
        pl.semaphore_signal(barrier, inc=1, device_id=(pz * NY + y, ps), device_id_type=MESH)
        return carry

    lax.fori_loop(1, PEERS, greet, 0, unroll=7)
    for n in (right, leftd):
        pl.semaphore_signal(barrier, inc=1, device_id=(n, s), device_id_type=MESH)
    whiten(wave, valid, basis, *scratch[-6:])
    pl.semaphore_wait(barrier, PEERS + 1)

    def cut(ref, where):
        part, lane = where
        lead = (slice(None),) * (len(ref.shape) - 3)
        if lane is None:
            return ref.at[lead + (part,)]
        return ref.at[lead + (part, slice(None), pl.ds(lane, 128))]

    def scatter(b, q):
        where = CUTS[b][q]

        def send(d, carry):
            pz, ps = peer(d)
            pltpu.make_async_remote_copy(
                src_ref=cut(white.at[ps * BINS + b], where),
                dst_ref=cut(spec[b].at[2 + zh, s], where),
                send_sem=send1.at[b, q],
                recv_sem=recv1.at[b, q],
                device_id=(pz * NY + y, ps),
                device_id_type=MESH,
            ).start()
            return carry

        lax.fori_loop(1, PEERS, send, 0, unroll=7)
        pltpu.make_async_copy(
            cut(white.at[s * BINS + b], where), cut(spec[b].at[2 + zh, s], where), recv1.at[b, q]
        ).start()

    def scatter_arrived(b, q):
        own = cut(spec[b].at[pl.ds(2, 2)], CUTS[b][q])
        pltpu.make_async_copy(own, own, recv1.at[b, q]).wait()

    def scatter_left(b, q):
        some = cut(white.at[pl.ds(0, PEERS - 1)], CUTS[b][q])
        pltpu.make_async_copy(some, some, send1.at[b, q]).wait()

    def neighbour(b, q, side):
        to, at = ((right, 0), (leftd, 4))[side]
        return pltpu.make_async_remote_copy(
            src_ref=cut(spec[b].at[pl.ds(2, 2)], CUTS[b][q]),
            dst_ref=cut(spec[b].at[pl.ds(at, 2)], CUTS[b][q]),
            send_sem=send2.at[b, q, side],
            recv_sem=recv2.at[b, q, side],
            device_id=(to, s),
            device_id_type=MESH,
        )

    def gift(b, side):
        to, group = ((right, lax.rem(y + 3, NY)), (leftd, NY + lax.rem(y + 1, NY)))[side]
        return pltpu.make_async_remote_copy(
            src_ref=give.at[b, side],
            dst_ref=res[b].at[group],
            send_sem=send3.at[b, side],
            recv_sem=recv3.at[b, side],
            device_id=(to, s),
            device_id_type=MESH,
        )

    def multiply(b):
        transpose_left(spec[b], 4 + zh, left)
        give[b, 0] = product(left, spec[b], 0)
        gift(b, 0).start()
        transpose_left(spec[b], zh, left)
        give[b, 1] = product(left, spec[b], 5)
        gift(b, 1).start()
        transpose_left(spec[b], 2 + zh, left)

        def block(t, carry):
            group = lax.rem(t, 2) * NY + lax.rem(y + 3 + lax.div(t, 2), NY)
            res[b][group] = product(left, spec[b], t)
            return carry

        lax.fori_loop(0, 6, block, 0)

    def assemble(b):
        def tile(m, carry):
            interleave(plan_ref, g, res[b], mid.at[b], tmp, m)
            return carry

        lax.fori_loop(0, 2 * G // TILE, tile, 0)

    def finish(b):
        for q in range(len(CUTS[b])):
            for side in range(2):
                neighbour(b, q, side).wait_recv()
        multiply(b)
        if b >= 1:
            for side in range(2):
                gift(b - 1, side).wait_recv()
            assemble(b - 1)

    steps = [(b, q) for b in range(BINS) for q in range(len(CUTS[b]))]
    ahead = AHEAD
    for b, q in steps[:ahead]:
        scatter(b, q)
    for k, (b, q) in enumerate(steps):
        scatter_arrived(b, q)
        for side in range(2):
            neighbour(b, q, side).start()
        while ahead < len(steps) and ahead <= k + AHEAD:
            scatter(*steps[ahead])
            ahead += 1
        if b >= 1 and q == 0:
            finish(b - 1)
    finish(LAST)
    for side in range(2):
        gift(LAST, side).wait_recv()
    for b, q in steps:
        scatter_left(b, q)
        for side in range(2):
            neighbour(b, q, side).wait_send()
    for b in range(BINS):
        for side in range(2):
            gift(b, side).wait_send()


def cross(plan, waveform, valid_count):
    bf16 = jnp.bfloat16
    samples = waveform.shape[-1]
    most = max(len(c) for c in CUTS)
    return pl.pallas_call(
        kernel,
        out_shape=(
            pltpu.VMEM((LAST, 2 * G * NGRP, G), bf16),
            pltpu.VMEM((NGRP, 2 * G, G), bf16),
        ),
        in_specs=[
            pl.BlockSpec(memory_space=pltpu.SMEM),
            pl.BlockSpec(memory_space=pl.ANY),
            pl.BlockSpec(memory_space=pltpu.VMEM),
            pl.BlockSpec(memory_space=pltpu.VMEM),
        ],
        out_specs=(pl.BlockSpec(memory_space=pltpu.VMEM),) * 2,
        scratch_shapes=[pltpu.VMEM((6, NS, 2, TILE, G), bf16)] * BINS
        + [pltpu.VMEM((NGRP, 2 * G, G), bf16)] * LAST
        + [
            pltpu.VMEM((BINS, 2, 2 * G, G), bf16),
            pltpu.VMEM((2 * G, DEPTH), bf16),
            pltpu.VMEM((2, TILE * NGRP, 128), jnp.float32),
            pltpu.SemaphoreType.DMA((BINS, most)),
            pltpu.SemaphoreType.DMA((BINS, most)),
            pltpu.SemaphoreType.DMA((BINS, most, 2)),
            pltpu.SemaphoreType.DMA((BINS, most, 2)),
            pltpu.SemaphoreType.DMA((BINS, 2)),
            pltpu.SemaphoreType.DMA((BINS, 2)),
            pltpu.VMEM((F, 2, TILE, G), bf16),
            pltpu.VMEM((G, TILE, samples), bf16),
            pltpu.VMEM((2, G // CHUNKS * TILE, 128), jnp.float32),
            pltpu.VMEM((2, F * TILE, G // CHUNKS), jnp.float32),
            pltpu.VMEM((G, TILE), jnp.int32),
            pltpu.SemaphoreType.DMA((G // PIECE,)),
        ],
        compiler_params=pltpu.CompilerParams(
            collective_id=0, has_side_effects=True, vmem_limit_bytes=52 * 1024 * 1024
        ),
    )(plan, waveform, valid_count.T, make_basis(samples))


QUARTERS = 4


def place_kernel(plan, mid, last, out, plan_ref, target, tmp, plan_sem, mid_sem, out_sem):
    g = lax.axis_index("grp")

    def keep(b):
        return pltpu.make_async_copy(mid.at[b], out.at[b], mid_sem.at[b])

    fetch = pltpu.make_async_copy(plan, plan_ref, plan_sem)
    fetch.start()
    for b in range(LAST):
        keep(b).start()
    fetch.wait()
    size = 2 * G * NGRP // QUARTERS

    def store(q):
        rows = pl.ds(q * size, size)
        return pltpu.make_async_copy(target.at[rows], out.at[LAST, rows], out_sem.at[q])

    def tile(m, carry):
        interleave(plan_ref, g, last, target, tmp, m)
        return carry

    each = 2 * G // TILE // QUARTERS
    for q in range(QUARTERS):
        lax.fori_loop(q * each, (q + 1) * each, tile, 0)
        store(q).start()
    for q in range(QUARTERS):
        store(q).wait()
    for b in range(LAST):
        keep(b).wait()


def place(plan, mid, last):
    bf16 = jnp.bfloat16
    return pl.pallas_call(
        place_kernel,
        out_shape=jax.ShapeDtypeStruct((BINS, 2 * G * NGRP, G), bf16),
        in_specs=[
            pl.BlockSpec(memory_space=pltpu.HBM),
            pl.BlockSpec(memory_space=pltpu.VMEM),
            pl.BlockSpec(memory_space=pltpu.VMEM),
        ],
        out_specs=pl.BlockSpec(memory_space=pl.ANY),
        scratch_shapes=[
            pltpu.SMEM((NGRP, plan.shape[1]), jnp.int32),
            pltpu.VMEM((2 * G * NGRP, G), bf16),
            pltpu.VMEM((2, TILE * NGRP, 128), jnp.float32),
            pltpu.SemaphoreType.DMA,
            pltpu.SemaphoreType.DMA((LAST,)),
            pltpu.SemaphoreType.DMA((QUARTERS,)),
        ],
        compiler_params=pltpu.CompilerParams(vmem_limit_bytes=16 * 1024 * 1024),
    )(
        pltpu.with_memory_space_constraint(plan, pltpu.HBM),
        pltpu.with_memory_space_constraint(mid, pltpu.VMEM),
        pltpu.with_memory_space_constraint(last, pltpu.VMEM),
    )


def shards(waveform, valid_count, plan):
    mid, last = cross(plan, waveform, valid_count)
    return place(plan, mid, last).reshape(BINS, 2, G, NGRP, G)


def solution(mesh):
    return jax.shard_map(
        shards,
        mesh=mesh,
        in_specs=(P("grp", "seg", None), P("grp", "seg"), P()),
        out_specs=P("seg", None, "grp", None, None),
        check_vma=False,
    )
```
